512 devices in a mesh: chan: 128 (over x, z, core), row: 4 (over y).
Axes of the slice: x: 4, y: 4, z: 16, core: 2. Of those that a mesh axis runs over, the one named last changes fastest.
Arguments:
- amplitudes: bfloat16 [2048, 128, 640], P('row', 'chan'), may hold values from -6 to 6
- block_rows: int32 [128], P('chan'), may hold values from 256 to 2048, as said below
- recoupling: bfloat16 [128, 128], replicated, may hold values from -1 to 2
- interaction: bfloat16 [2048, 128, 2048], P(None, 'chan', 'row'), may hold values from -0.125 to 0.125
Outputs:
- residual: bfloat16 [2048, 128, 640], P('row', 'chan')
The draws below stay inside these ranges and needn't reach their ends.
Inputs may be any that keep to these rules, and one draw needn't show every extreme that they name: `block_rows`: each entry is at least 256 and at most 2048; some channel has exactly 2048 live rows.
All inputs are finite; a program needn't handle non-finite values.
Results may differ from the reference program's by a relative error of at most 0.015.
Values may be sent and summed in bfloat16 or wider, within the bound.
A program may use at most 64 MiB of HBM per device.

```python
import math
import jax
import jax.numpy as jnp
from jax import lax

P_SIZE = 2048
Q = 640
NJ = 128
N_ROW = 4


def draw_block_rows(key, part):
    key = jax.random.fold_in(key, 11)
    first_key, second_key = jax.random.split(key)
    lengths = jax.random.randint(first_key, (NJ,), P_SIZE // 8, P_SIZE + 1, dtype=jnp.int32)
    largest_channel = jax.random.randint(second_key, (), 0, NJ, dtype=jnp.int32)
    return lengths.at[largest_channel].set(P_SIZE)


def draw_recoupling(key, part):
    key = jax.random.fold_in(key, 12)
    spread = jnp.clip(jax.random.normal(key, (NJ, NJ), jnp.float32), -4.0, 4.0) * 0.5
    matrix = jnp.eye(NJ, dtype=jnp.float32) + spread / math.sqrt(NJ)
    return matrix.astype(jnp.bfloat16)


def shard_levels(own_key, dims, pieces, least, largest):
    def one(dim, shards_of):
        draws = jax.random.uniform(jax.random.fold_in(jax.random.fold_in(own_key, 6), dim), (shards_of,), jnp.float32, least / len(pieces), largest / len(pieces))
        return jnp.repeat(jnp.exp(draws), dims[dim] // shards_of).reshape((-1,) + (1,) * (len(dims) - dim - 1))

    gain = one(*pieces[0])
    for cut in pieces[1:]:
        gain = gain * one(*cut)
    return gain


def noise(rng, shape, scale, bound, pieces=(), kind=jnp.bfloat16):
    gain = shard_levels(rng, shape, pieces, -0.22, 0.18) if pieces else 1.0
    array = jax.random.normal(rng, shape, jnp.float32) * scale * gain
    return jnp.minimum(jnp.maximum(array, -bound), bound).astype(kind)


def setup_inputs(seed: int = 0) -> dict:
    keys = jax.random.split(jax.random.key(seed), 5)
    return {
        "amplitudes": noise(keys[0], (P_SIZE, NJ, Q), 1.0, 6.0, ((0, 4), (1, 128))),
        "block_rows": draw_block_rows(jax.random.fold_in(keys[4], 71), 0),
        "recoupling": draw_recoupling(jax.random.fold_in(keys[4], 71), 0),
        "interaction": noise(keys[3], (P_SIZE, NJ, P_SIZE), P_SIZE ** -0.5, 0.125, ((1, 128), (2, 4))),
    }


def recouple(data, matrix, pattern):
    block_len = 32
    blocks = data.reshape(P_SIZE // block_len, block_len, NJ, Q)
    wide = matrix.astype(jnp.float32)

    def one_block(row_block):
        return jnp.einsum(pattern, wide, row_block.astype(jnp.float32), precision=lax.Precision.HIGHEST).astype(jnp.bfloat16)

    return lax.map(one_block, blocks).reshape(P_SIZE, NJ, Q)


def reference(amplitudes, block_rows, recoupling, interaction):
    row_identifiers = jnp.arange(P_SIZE, dtype=jnp.int32)
    live = row_identifiers[:, None] < block_rows[None, :]
    zero = jnp.zeros((), jnp.bfloat16)
    masked = jnp.where(live[:, :, None], amplitudes, zero)
    cross = recouple(masked, recoupling, "kj,rjq->rkq")
    grouped_row_list = P_SIZE // N_ROW

    def cycle_channel(chan_id):
        weights = lax.dynamic_index_in_dim(interaction, chan_id, 1, keepdims=False)
        cross_block = lax.dynamic_index_in_dim(cross, chan_id, 1, keepdims=False)
        weights = weights.reshape(P_SIZE, N_ROW, grouped_row_list).astype(jnp.float32)
        cross_block = cross_block.reshape(N_ROW, grouped_row_list, Q).astype(jnp.float32)
        partials = jnp.einsum("pkr,krq->kpq", weights, cross_block, precision=lax.Precision.HIGHEST)
        rounded = lax.optimization_barrier(partials.astype(jnp.bfloat16)).astype(jnp.float32)
        return jnp.sum(rounded, axis=0).astype(jnp.bfloat16)

    reduced_total = lax.map(cycle_channel, jnp.arange(NJ, dtype=jnp.int32))
    reduced_total = jnp.moveaxis(reduced_total, 0, 1)
    back = recouple(reduced_total, recoupling, "jk,rjq->rkq")
    return jnp.where(live[:, :, None], back, zero)
```

```python
import jax
import jax.numpy as jnp
from jax import lax
from jax.experimental import pallas as pl
from jax.experimental.pallas import tpu as pltpu
from jax.sharding import PartitionSpec as P

MESH = pl.DeviceIdType.MESH
BF = jnp.bfloat16
F32 = jnp.float32

NX, NZ, NC, NY = 4, 16, 2, 4
NG = NX * NC
NCHAN = NG * NZ
ROWS = 512
SUB = ROWS // NCHAN
GB, ZB = ROWS // NG, ROWS // NZ
Q = 640
WIDTHS = (128,) * 5
STARTS = tuple(sum(WIDTHS[:i]) for i in range(len(WIDTHS)))
C = len(WIDTHS)

N_STEP = 10
BUFS = ("xs", "xr", "zs", "zr", "ms", "mr", "ps", "pr", "ss", "xr2", "zs2", "zr2", "ms2", "mr2", "ps2", "pr2")


def make_order():
    order = []
    for t in range(N_STEP + 2 * (C - 1)):
        for c in range(C):
            s = t - 2 * c
            if 0 <= s < N_STEP:
                order.append((s, c))
    return order


ORDER = make_order()


def chan_of_row(r):
    z, g = r // (NG * SUB), (r // SUB) % NG
    return ((g // NC) * NZ + z) * NC + g % NC


def dot(a, b):
    return lax.dot_general(a, b, (((1,), (0,)), ((), ())), preferred_element_type=F32)


def dot_nt(a, b):
    return lax.dot_general(a, b, (((1,), (1,)), ((), ())), preferred_element_type=F32)


def kernel(len_ref, amp_ref, rec_ref, int_ref, out_ref, *refs):
    bufs = []
    n = len(BUFS) + 2
    for c in range(C):
        mine = refs[c * n : (c + 1) * n]
        bufs.append(dict(zip(BUFS + ("ts", "tr"), mine)))
    inter, k1, k2, p1, p2, recv, send, load = refs[C * n :]

    chan, y = lax.axis_index("chan"), lax.axis_index("row")
    core, z, x = chan % NC, (chan // NC) % NZ, chan // (NC * NZ)
    g = x * NC + core

    def at_group(peer):
        return (((peer // NC) * NZ + z) * NC + peer % NC, y)

    def at_z(peer):
        return ((x * NZ + peer) * NC + core, y)

    def at_y(peer):
        return (chan, peer)

    barrier = pltpu.get_barrier_semaphore()

    def hail(count, me, where):
        def body(i, carry):
            pl.semaphore_signal(barrier, inc=1, device_id=where((me + i) % count), device_id_type=MESH)
            return carry

        lax.fori_loop(1, count, body, 0)

    hail(NG, g, at_group)
    hail(NZ, z, at_z)
    hail(NY, y, at_y)

    fetch = pltpu.make_async_copy(int_ref, inter, load)
    fetch.start()

    live = len_ref[0] - y * ROWS

    def masked(value):
        rows = lax.broadcasted_iota(jnp.int32, value.shape, 0)
        return jnp.where(rows < live, value.astype(F32), 0.0).astype(BF)

    def build():
        r = lax.broadcasted_iota(jnp.int32, (ROWS, NCHAN), 0)
        k = lax.broadcasted_iota(jnp.int32, (ROWS, NCHAN), 1)
        pick = (chan_of_row(r) == k).astype(F32).astype(BF)
        a = lax.broadcasted_iota(jnp.int32, (ROWS, ROWS), 0)
        b = lax.broadcasted_iota(jnp.int32, (ROWS, ROWS), 1)
        same = (a % SUB) == (b % SUB)
        rec = rec_ref[...]
        k1[...] = jnp.where(same, dot_nt(dot(pick, rec).astype(BF), pick), 0.0).astype(BF)
        k2[...] = jnp.where(same, dot_nt(dot_nt(pick, rec).astype(BF), pick), 0.0).astype(BF)
        there = ((a // SUB) % NG) * GB + (a // ZB) * SUB + a % SUB
        p1[...] = (there == b).astype(F32).astype(BF)
        back = ((b // SUB) % NG) * GB + (b // ZB) * SUB + b % SUB
        p2[...] = (back == a).astype(F32).astype(BF)

    def swap(stage, c, src, dst, count, me, rows, where):
        own = pl.ds(pl.multiple_of(me * rows, rows), rows)
        pltpu.make_async_copy(src.at[own], dst.at[own], recv.at[stage, c]).start()

        def body(i, carry):
            if count == NZ:
                odd = i % 2
                step = NZ // 2 + (1 - odd) * (i // 2) - odd * ((i + 1) // 2)
            else:
                step = i + 1
            peer = (me + step) % count
            pltpu.make_async_remote_copy(
                src_ref=src.at[pl.ds(pl.multiple_of(peer * rows, rows), rows)],
                dst_ref=dst.at[own],
                send_sem=send.at[stage, c],
                recv_sem=recv.at[stage, c],
                device_id=where(peer),
                device_id_type=MESH,
            ).start()
            return carry

        lax.fori_loop(0, count - 1, body, 0)

    def swap_group(stage, c, src, dst):
        swap(stage, c, bufs[c][src], bufs[c][dst], NG, g, GB, at_group)

    def swap_z(stage, c, src, dst):
        swap(stage, c, bufs[c][src], bufs[c][dst], NZ, z, ZB, at_z)

    def arrived(stage, c, dst):
        ref = bufs[c][dst]
        pltpu.make_async_copy(ref, ref, recv.at[stage, c]).wait()
        return ref

    def step(s, c):
        b, w = bufs[c], WIDTHS[c]
        cols = pl.ds(STARTS[c], w)
        if s == 0:
            b["xs"][...] = masked(amp_ref[:, cols])
            swap_group(0, c, "xs", "xr")
        elif s == 1:
            b["zs"][...] = dot(p1[...], arrived(0, c, "xr")[...]).astype(BF)
            swap_z(1, c, "zs", "zr")
        elif s == 2:
            b["ms"][...] = dot(k1[...], arrived(1, c, "zr")[...]).astype(BF)
            swap_z(2, c, "ms", "mr")
        elif s == 3:
            b["ps"][...] = dot(p2[...], arrived(2, c, "mr")[...]).astype(BF)
            swap_group(3, c, "ps", "pr")
        elif s == 4:
            cross = arrived(3, c, "pr")
            if c == 0:
                fetch.wait()

            def body(i, carry):
                peer = (y + 1 + i) % NY
                rows = pl.ds(pl.multiple_of(peer * ROWS, ROWS), ROWS)
                b["ts"][rows, :] = dot(inter[rows, :], cross[...]).astype(BF)

                @pl.when(i < NY - 1)
                def _():
                    pltpu.make_async_remote_copy(
                        src_ref=b["ts"].at[rows],
                        dst_ref=b["tr"].at[pl.ds(pl.multiple_of(i * ROWS, ROWS), ROWS)],
                        send_sem=send.at[4, c],
                        recv_sem=recv.at[4, c],
                        device_id=at_y(peer),
                        device_id_type=MESH,
                    ).start()

                return carry

            lax.fori_loop(0, NY, body, 0)
        elif s == 5:
            tr = arrived(4, c, "tr")
            total = b["ts"][pl.ds(pl.multiple_of(y * ROWS, ROWS), ROWS), :].astype(F32)
            for i in range(NY - 1):
                total = total + tr[pl.ds(i * ROWS, ROWS), :].astype(F32)
            b["ss"][...] = total.astype(BF)
            swap_group(5, c, "ss", "xr2")
        elif s == 6:
            b["zs2"][...] = dot(p1[...], arrived(5, c, "xr2")[...]).astype(BF)
            swap_z(6, c, "zs2", "zr2")
        elif s == 7:
            b["ms2"][...] = dot(k2[...], arrived(6, c, "zr2")[...]).astype(BF)
            swap_z(7, c, "ms2", "mr2")
        elif s == 8:
            b["ps2"][...] = dot(p2[...], arrived(7, c, "mr2")[...]).astype(BF)
            swap_group(8, c, "ps2", "pr2")
        else:
            out_ref[:, cols] = masked(arrived(8, c, "pr2")[...])

    pl.semaphore_wait(barrier, NG + NZ + NY - 3)
    for i, (s, c) in enumerate(ORDER):
        step(s, c)
        if i == 0:
            build()

    def sent(stage, c, ref, rows):
        part = ref.at[pl.ds(0, rows)]
        pltpu.make_async_copy(part, part, send.at[stage, c]).wait()

    for c in range(C):
        for stage in range(9):
            if stage == 4:
                sent(stage, c, bufs[c]["ts"], ROWS * (NY - 1))
            elif stage in (0, 3, 5, 8):
                sent(stage, c, bufs[c]["xs"], ROWS - GB)
            else:
                sent(stage, c, bufs[c]["xs"], ROWS - ZB)


def on_device(amplitudes, block_rows, recoupling, interaction):
    amp = amplitudes.reshape(ROWS, Q)
    inter = interaction.reshape(NY * ROWS, ROWS)
    scratch = []
    for w in WIDTHS:
        scratch += [pltpu.VMEM((ROWS, w), BF)] * len(BUFS)
        scratch += [pltpu.VMEM((NY * ROWS, w), BF), pltpu.VMEM(((NY - 1) * ROWS, w), BF)]
    scratch += [pltpu.VMEM((NY * ROWS, ROWS), BF)]
    scratch += [pltpu.VMEM((ROWS, ROWS), BF)] * 4
    scratch += [pltpu.SemaphoreType.DMA((9, C)), pltpu.SemaphoreType.DMA((9, C)), pltpu.SemaphoreType.DMA]
    out = pl.pallas_call(
        kernel,
        out_shape=jax.ShapeDtypeStruct((ROWS, Q), BF),
        in_specs=[
            pl.BlockSpec(memory_space=pltpu.SMEM),
            pl.BlockSpec(memory_space=pltpu.VMEM),
            pl.BlockSpec(memory_space=pltpu.VMEM),
            pl.BlockSpec(memory_space=pl.ANY),
        ],
        out_specs=pl.BlockSpec(memory_space=pltpu.VMEM),
        scratch_shapes=scratch,
        compiler_params=pltpu.CompilerParams(
            collective_id=0, has_side_effects=True, vmem_limit_bytes=48 * 1024 * 1024
        ),
        cost_estimate=pl.CostEstimate(flops=4 * 10**9, bytes_accessed=4 * 10**6, transcendentals=0),
    )(block_rows, amp, recoupling, inter)
    return out.reshape(ROWS, 1, Q)


def solution(mesh):
    return jax.shard_map(
        on_device,
        mesh=mesh,
        in_specs=(P("row", "chan", None), P("chan"), P(), P(None, "chan", "row")),
        out_specs=P("row", "chan", None),
        check_vma=False,
    )
```

```python
import jax
import jax.numpy as jnp
from jax import lax
from jax.experimental import pallas as pl
from jax.experimental.pallas import tpu as pltpu
from jax.sharding import PartitionSpec as P

MESH = pl.DeviceIdType.MESH
BF = jnp.bfloat16
F32 = jnp.float32

NX, NZ, NC, NY = 4, 16, 2, 4
NG = NX * NC
NCHAN = NG * NZ
ROWS = 512
SUB = ROWS // NCHAN
GB, ZB = ROWS // NG, ROWS // NZ
Q = 640
WIDTHS = (128,) * 5
STARTS = tuple(sum(WIDTHS[:i]) for i in range(len(WIDTHS)))
C = len(WIDTHS)

ORDER = (
    (0, 0), (0, 1), (0, 2), (1, 0), (0, 3), (2, 0), (1, 1), (0, 4), (2, 1), (1, 2),
    (3, 0), (2, 2), (1, 3), (3, 1), (2, 3), (1, 4), (3, 2), (2, 4), (4, 0), (3, 3),
    (4, 1), (3, 4), (4, 2), (5, 0), (4, 3), (5, 1), (4, 4), (5, 2), (6, 0), (5, 3),
    (7, 0), (6, 1), (5, 4), (7, 1), (6, 2), (8, 0), (7, 2), (6, 3), (8, 1), (7, 3),
    (6, 4), (8, 2), (7, 4), (9, 0), (8, 3), (9, 1), (8, 4), (9, 2), (9, 3), (9, 4),
)

BUFS = ("z1", "z1r", "x1", "x1r", "x2", "x2r", "z2", "z2r", "z3", "z3r", "x3", "x3r", "x4", "x4r", "z4")
N_STAGE = 9


def chan_of_row(r):
    g, z = r // GB, (r // SUB) % NZ
    return ((g // NC) * NZ + z) * NC + g % NC


def dot(a, b):
    return lax.dot_general(a, b, (((1,), (0,)), ((), ())), preferred_element_type=F32)


def dot_nt(a, b):
    return lax.dot_general(a, b, (((1,), (1,)), ((), ())), preferred_element_type=F32)


def kernel(length, amp_any, rec_any, int_any, out_any, *refs):
    bufs = []
    n = len(BUFS) + 2
    for c in range(C):
        bufs.append(dict(zip(BUFS + ("ts", "tr"), refs[c * n : (c + 1) * n])))
    amp, inter, rec, k1, k2, p1, p2, recv, send, load = refs[C * n :]

    loads = []
    for c in range(C):
        cols = pl.ds(STARTS[c], WIDTHS[c])
        loads.append(pltpu.make_async_copy(amp_any.at[:, cols], amp.at[:, cols], load.at[c]))
    loads.append(pltpu.make_async_copy(rec_any, rec, load.at[C]))
    loads.append(pltpu.make_async_copy(int_any, inter, load.at[C + 1]))
    for copy in loads:
        copy.start()

    chan, y = lax.axis_index("chan"), lax.axis_index("row")
    core, z, x = chan % NC, (chan // NC) % NZ, chan // (NC * NZ)
    g = x * NC + core

    def at_group(peer):
        return (((peer // NC) * NZ + z) * NC + peer % NC, y)

    def at_z(peer):
        return ((x * NZ + peer) * NC + core, y)

    def at_y(peer):
        return (chan, peer)

    barrier = pltpu.get_barrier_semaphore()

    def hail(count, me, where):
        def body(i, carry):
            pl.semaphore_signal(barrier, inc=1, device_id=where((me + i) % count), device_id_type=MESH)
            return carry

        lax.fori_loop(1, count, body, 0)

    hail(NZ, z, at_z)
    hail(NG, g, at_group)
    hail(NY, y, at_y)

    def mask_in(c):
        loads[c].wait()
        value = amp[:, pl.ds(STARTS[c], WIDTHS[c])]
        rows = lax.broadcasted_iota(jnp.int32, value.shape, 0)
        live = rows < length[0] - y * ROWS
        bufs[c]["z1"][...] = jnp.where(live, value.astype(F32), 0.0).astype(BF)

    def build():
        r = lax.broadcasted_iota(jnp.int32, (ROWS, NCHAN), 0)
        k = lax.broadcasted_iota(jnp.int32, (ROWS, NCHAN), 1)
        pick = (chan_of_row(r) == k).astype(F32).astype(BF)
        a = lax.broadcasted_iota(jnp.int32, (ROWS, ROWS), 0)
        b = lax.broadcasted_iota(jnp.int32, (ROWS, ROWS), 1)
        same = (a % SUB) == (b % SUB)
        there = ((a // SUB) % NZ) * ZB + (a // GB) * SUB + a % SUB
        p1[...] = (there == b).astype(F32).astype(BF)
        back = ((b // SUB) % NZ) * ZB + (b // GB) * SUB + b % SUB
        p2[...] = (back == a).astype(F32).astype(BF)
        loads[C].wait()
        coef = rec[...]
        k1[...] = jnp.where(same, dot_nt(dot(pick, coef).astype(BF), pick), 0.0).astype(BF)
        k2[...] = jnp.where(same, dot_nt(dot_nt(pick, coef).astype(BF), pick), 0.0).astype(BF)

    def swap(stage, c, src, dst, count, me, rows, where):
        own = pl.ds(pl.multiple_of(me * rows, rows), rows)
        pltpu.make_async_copy(src.at[own], dst.at[own], recv.at[stage, c]).start()

        def body(i, carry):
            if count == NZ:
                odd = i % 2
                step = NZ // 2 + (1 - odd) * (i // 2) - odd * ((i + 1) // 2)
            else:
                step = i + 1
            peer = (me + step) % count
            pltpu.make_async_remote_copy(
                src_ref=src.at[pl.ds(pl.multiple_of(peer * rows, rows), rows)],
                dst_ref=dst.at[own],
                send_sem=send.at[stage, c],
                recv_sem=recv.at[stage, c],
                device_id=where(peer),
                device_id_type=MESH,
            ).start()
            return carry

        lax.fori_loop(0, count - 1, body, 0)

    def swap_group(stage, c, src, dst):
        swap(stage, c, bufs[c][src], bufs[c][dst], NG, g, GB, at_group)

    def out_cols(c):
        return out_any.at[:, pl.ds(STARTS[c], WIDTHS[c])]

    def swap_z(stage, c, src, dst):
        to = bufs[c][dst] if dst else out_cols(c)
        swap(stage, c, bufs[c][src], to, NZ, z, ZB, at_z)

    def arrived(stage, c, dst):
        ref = bufs[c][dst] if dst else out_cols(c)
        pltpu.make_async_copy(ref, ref, recv.at[stage, c]).wait()
        return ref

    def step(s, c):
        b = bufs[c]
        if s == 0:
            mask_in(c)
            swap_z(0, c, "z1", "z1r")
        elif s == 1:
            b["x1"][...] = dot(p1[...], arrived(0, c, "z1r")[...]).astype(BF)
            swap_group(1, c, "x1", "x1r")
        elif s == 2:
            b["x2"][...] = dot(k1[...], arrived(1, c, "x1r")[...]).astype(BF)
            swap_group(2, c, "x2", "x2r")
        elif s == 3:
            b["z2"][...] = dot(p2[...], arrived(2, c, "x2r")[...]).astype(BF)
            swap_z(3, c, "z2", "z2r")
        elif s == 4:
            cross = arrived(3, c, "z2r")
            if c == 0:
                loads[C + 1].wait()

            def body(i, carry):
                peer = (y + 1 + i) % NY
                rows = pl.ds(pl.multiple_of(peer * ROWS, ROWS), ROWS)
                b["ts"][rows, :] = dot(inter[rows, :], cross[...]).astype(BF)

                @pl.when(i < NY - 1)
                def _():
                    pltpu.make_async_remote_copy(
                        src_ref=b["ts"].at[rows],
                        dst_ref=b["tr"].at[pl.ds(pl.multiple_of(i * ROWS, ROWS), ROWS)],
                        send_sem=send.at[4, c],
                        recv_sem=recv.at[4, c],
                        device_id=at_y(peer),
                        device_id_type=MESH,
                    ).start()

                return carry

            lax.fori_loop(0, NY, body, 0)
        elif s == 5:
            tr = arrived(4, c, "tr")
            total = b["ts"][pl.ds(pl.multiple_of(y * ROWS, ROWS), ROWS), :].astype(F32)
            for i in range(NY - 1):
                total = total + tr[pl.ds(i * ROWS, ROWS), :].astype(F32)
            b["z3"][...] = total.astype(BF)
            swap_z(5, c, "z3", "z3r")
        elif s == 6:
            b["x3"][...] = dot(p1[...], arrived(5, c, "z3r")[...]).astype(BF)
            swap_group(6, c, "x3", "x3r")
        elif s == 7:
            b["x4"][...] = dot(k2[...], arrived(6, c, "x3r")[...]).astype(BF)
            swap_group(7, c, "x4", "x4r")
        elif s == 8:
            b["z4"][...] = dot(p2[...], arrived(7, c, "x4r")[...]).astype(BF)
            swap_z(8, c, "z4", None)
        else:
            arrived(8, c, None)

    pl.semaphore_wait(barrier, NG + NZ + NY - 3)
    for i, (s, c) in enumerate(ORDER):
        step(s, c)
        if i == 1:
            build()

    def sent(stage, c, ref, rows):
        part = ref.at[pl.ds(0, rows)]
        pltpu.make_async_copy(part, part, send.at[stage, c]).wait()

    for c in range(C):
        for stage in range(N_STAGE):
            if stage == 4:
                sent(stage, c, bufs[c]["ts"], ROWS * (NY - 1))
            elif stage in (0, 3, 5, 8):
                sent(stage, c, bufs[c]["z1"], ROWS - ZB)
            else:
                sent(stage, c, bufs[c]["z1"], ROWS - GB)


def on_device(amplitudes, block_rows, recoupling, interaction):
    amp = amplitudes.reshape(ROWS, Q)
    inter = interaction.reshape(NY * ROWS, ROWS)
    scratch = []
    for w in WIDTHS:
        scratch += [pltpu.VMEM((ROWS, w), BF)] * len(BUFS)
        scratch += [pltpu.VMEM((NY * ROWS, w), BF), pltpu.VMEM(((NY - 1) * ROWS, w), BF)]
    scratch += [pltpu.VMEM((ROWS, Q), BF), pltpu.VMEM((NY * ROWS, ROWS), BF), pltpu.VMEM((NCHAN, NCHAN), BF)]
    scratch += [pltpu.VMEM((ROWS, ROWS), BF)] * 4
    scratch += [pltpu.SemaphoreType.DMA((N_STAGE, C)), pltpu.SemaphoreType.DMA((N_STAGE, C))]
    scratch += [pltpu.SemaphoreType.DMA((C + 2,))]
    out = pl.pallas_call(
        kernel,
        out_shape=jax.ShapeDtypeStruct((ROWS, Q), BF),
        in_specs=[pl.BlockSpec(memory_space=pltpu.SMEM)] + [pl.BlockSpec(memory_space=pl.ANY)] * 3,
        out_specs=pl.BlockSpec(memory_space=pl.ANY),
        scratch_shapes=scratch,
        compiler_params=pltpu.CompilerParams(
            collective_id=0, has_side_effects=True, vmem_limit_bytes=60 * 1024 * 1024
        ),
        cost_estimate=pl.CostEstimate(flops=4 * 10**9, bytes_accessed=4 * 10**6, transcendentals=0),
    )(block_rows, amp, recoupling, inter)
    rows = lax.axis_index("row") * ROWS + lax.iota(jnp.int32, ROWS)
    live = (rows[:, None] < block_rows[None, :])[:, :, None]
    return jnp.where(live, out.reshape(ROWS, 1, Q), jnp.zeros((), BF))


def solution(mesh):
    return jax.shard_map(
        on_device,
        mesh=mesh,
        in_specs=(P("row", "chan", None), P("chan"), P(), P(None, "chan", "row")),
        out_specs=P("row", "chan", None),
        check_vma=False,
    )
```

```python
import jax
import jax.numpy as jnp
from jax import lax
from jax.experimental import pallas as pl
from jax.experimental.pallas import tpu as pltpu
from jax.sharding import PartitionSpec as P

MESH = pl.DeviceIdType.MESH
BF = jnp.bfloat16
F32 = jnp.float32

NX, NZ, NC, NY = 4, 16, 2, 4
NG = NX * NC
NCHAN = NG * NZ
ROWS = 512
SUB = ROWS // NCHAN
GB, ZB = ROWS // NG, ROWS // NZ
Q = 640
WIDTHS = (128,) * 5
STARTS = tuple(sum(WIDTHS[:i]) for i in range(len(WIDTHS)))
C = len(WIDTHS)

ORDER = (
    (0, 0), (0, 1), (0, 2), (1, 0), (0, 3), (2, 0), (1, 1), (0, 4), (2, 1), (1, 2),
    (3, 0), (2, 2), (1, 3), (3, 1), (2, 3), (1, 4), (3, 2), (2, 4), (4, 0), (3, 3),
    (4, 1), (3, 4), (4, 2), (5, 0), (4, 3), (5, 1), (4, 4), (5, 2), (6, 0), (5, 3),
    (7, 0), (6, 1), (5, 4), (7, 1), (6, 2), (8, 0), (7, 2), (6, 3), (8, 1), (7, 3),
    (6, 4), (8, 2), (7, 4), (9, 0), (8, 3), (9, 1), (8, 4), (9, 2), (9, 3), (9, 4),
)

BUFS = ("z1", "z1r", "x1", "x1r", "x2", "x2r", "z2", "z2r", "z3", "z3r", "x3", "x3r", "x4", "x4r", "z4")
N_STAGE = 9


def chan_of_row(r):
    g, z = r // GB, (r // SUB) % NZ
    return ((g // NC) * NZ + z) * NC + g % NC


def dot(a, b):
    return lax.dot_general(a, b, (((1,), (0,)), ((), ())), preferred_element_type=F32)


def dot_nt(a, b):
    return lax.dot_general(a, b, (((1,), (1,)), ((), ())), preferred_element_type=F32)


def kernel(length, amp_any, rec_any, int_any, out_any, *refs):
    bufs = []
    n = len(BUFS) + 2
    for c in range(C):
        bufs.append(dict(zip(BUFS + ("ts", "tr"), refs[c * n : (c + 1) * n])))
    amp, inter, rec, k1, k2, p1, p2, recv, send, load = refs[C * n :]

    loads = []
    for c in range(C):
        cols = pl.ds(STARTS[c], WIDTHS[c])
        loads.append(pltpu.make_async_copy(amp_any.at[:, cols], amp.at[:, cols], load.at[c]))
    loads.append(pltpu.make_async_copy(rec_any, rec, load.at[C]))
    loads.append(pltpu.make_async_copy(int_any, inter, load.at[C + 1]))
    loads[0].start()

    chan, y = lax.axis_index("chan"), lax.axis_index("row")
    core, z, x = chan % NC, (chan // NC) % NZ, chan // (NC * NZ)
    g = x * NC + core

    def at_group(peer):
        return (((peer // NC) * NZ + z) * NC + peer % NC, y)

    def at_z(peer):
        return ((x * NZ + peer) * NC + core, y)

    def at_y(peer):
        return (chan, peer)

    barrier = pltpu.get_barrier_semaphore()

    def hail(count, me, where):
        for i in range(1, count):
            pl.semaphore_signal(barrier, inc=1, device_id=where((me + i) % count), device_id_type=MESH)

    hail(NZ, z, at_z)
    hail(NG, g, at_group)
    hail(NY, y, at_y)
    for copy in loads[1:]:
        copy.start()

    def mask_in(c):
        loads[c].wait()
        value = amp[:, pl.ds(STARTS[c], WIDTHS[c])]
        rows = lax.broadcasted_iota(jnp.int32, value.shape, 0)
        live = rows < length[0] - y * ROWS
        bufs[c]["z1"][...] = jnp.where(live, value.astype(F32), 0.0).astype(BF)

    def build():
        r = lax.broadcasted_iota(jnp.int32, (ROWS, NCHAN), 0)
        k = lax.broadcasted_iota(jnp.int32, (ROWS, NCHAN), 1)
        pick = (chan_of_row(r) == k).astype(F32).astype(BF)
        a = lax.broadcasted_iota(jnp.int32, (ROWS, ROWS), 0)
        b = lax.broadcasted_iota(jnp.int32, (ROWS, ROWS), 1)
        same = (a % SUB) == (b % SUB)
        there = ((a // SUB) % NZ) * ZB + (a // GB) * SUB + a % SUB
        p1[...] = (there == b).astype(F32).astype(BF)
        back = ((b // SUB) % NZ) * ZB + (b // GB) * SUB + b % SUB
        p2[...] = (back == a).astype(F32).astype(BF)
        loads[C].wait()
        coef = rec[...]
        k1[...] = jnp.where(same, dot_nt(dot(pick, coef).astype(BF), pick), 0.0).astype(BF)
        k2[...] = jnp.where(same, dot_nt(dot_nt(pick, coef).astype(BF), pick), 0.0).astype(BF)

    def swap(stage, c, src, dst, count, me, rows, where):
        own = pl.ds(pl.multiple_of(me * rows, rows), rows)
        pltpu.make_async_copy(src.at[own], dst.at[own], recv.at[stage, c]).start()

        def body(i, carry):
            if stage == 8 and c >= C - 2:
                peer = i + (i >= me).astype(jnp.int32)
            elif count == NZ:
                odd = i % 2
                peer = (me + NZ // 2 + (1 - odd) * (i // 2) - odd * ((i + 1) // 2)) % count
            else:
                peer = (me + i + 1) % count
            pltpu.make_async_remote_copy(
                src_ref=src.at[pl.ds(pl.multiple_of(peer * rows, rows), rows)],
                dst_ref=dst.at[own],
                send_sem=send.at[stage, c],
                recv_sem=recv.at[stage, c],
                device_id=where(peer),
                device_id_type=MESH,
            ).start()
            return carry

        lax.fori_loop(0, count - 1, body, 0)

    def swap_group(stage, c, src, dst):
        swap(stage, c, bufs[c][src], bufs[c][dst], NG, g, GB, at_group)

    def out_cols(c):
        return out_any.at[:, pl.ds(STARTS[c], WIDTHS[c])]

    def swap_z(stage, c, src, dst):
        to = bufs[c][dst] if dst else out_cols(c)
        swap(stage, c, bufs[c][src], to, NZ, z, ZB, at_z)

    def arrived(stage, c, dst):
        ref = bufs[c][dst] if dst else out_cols(c)
        pltpu.make_async_copy(ref, ref, recv.at[stage, c]).wait()
        return ref

    def step(s, c):
        b = bufs[c]
        if s == 0:
            if c:
                mask_in(c)
            swap_z(0, c, "z1", "z1r")
        elif s == 1:
            b["x1"][...] = dot(p1[...], arrived(0, c, "z1r")[...]).astype(BF)
            swap_group(1, c, "x1", "x1r")
        elif s == 2:
            b["x2"][...] = dot(k1[...], arrived(1, c, "x1r")[...]).astype(BF)
            swap_group(2, c, "x2", "x2r")
        elif s == 3:
            b["z2"][...] = dot(p2[...], arrived(2, c, "x2r")[...]).astype(BF)
            swap_z(3, c, "z2", "z2r")
        elif s == 4:
            cross = arrived(3, c, "z2r")
            if c == 0:
                loads[C + 1].wait()

            def body(i, carry):
                peer = (y + 1 + i) % NY
                rows = pl.ds(pl.multiple_of(peer * ROWS, ROWS), ROWS)
                b["ts"][rows, :] = dot(inter[rows, :], cross[...]).astype(BF)

                @pl.when(i < NY - 1)
                def _():
                    pltpu.make_async_remote_copy(
                        src_ref=b["ts"].at[rows],
                        dst_ref=b["tr"].at[pl.ds(pl.multiple_of(i * ROWS, ROWS), ROWS)],
                        send_sem=send.at[4, c],
                        recv_sem=recv.at[4, c],
                        device_id=at_y(peer),
                        device_id_type=MESH,
                    ).start()

                return carry

            lax.fori_loop(0, NY, body, 0)
        elif s == 5:
            tr = arrived(4, c, "tr")
            total = b["ts"][pl.ds(pl.multiple_of(y * ROWS, ROWS), ROWS), :].astype(F32)
            for i in range(NY - 1):
                total = total + tr[pl.ds(i * ROWS, ROWS), :].astype(F32)
            b["z3"][...] = total.astype(BF)
            swap_z(5, c, "z3", "z3r")
        elif s == 6:
            b["x3"][...] = dot(p1[...], arrived(5, c, "z3r")[...]).astype(BF)
            swap_group(6, c, "x3", "x3r")
        elif s == 7:
            b["x4"][...] = dot(k2[...], arrived(6, c, "x3r")[...]).astype(BF)
            swap_group(7, c, "x4", "x4r")
        elif s == 8:
            b["z4"][...] = dot(p2[...], arrived(7, c, "x4r")[...]).astype(BF)
            swap_z(8, c, "z4", None)
        else:
            arrived(8, c, None)

    def sent(stage, c):
        rows = ROWS * (NY - 1) if stage == 4 else ROWS - (ZB if stage in (0, 3, 5, 8) else GB)
        part = bufs[c]["ts"].at[pl.ds(0, rows)]
        pltpu.make_async_copy(part, part, send.at[stage, c]).wait()

    mask_in(0)
    pl.semaphore_wait(barrier, NG + NZ + NY - 3)
    for i, (s, c) in enumerate(ORDER):
        step(s, c)
        if s >= 2:
            sent(s - 2, c)
        if i == 1:
            build()
    for c in range(C):
        sent(N_STAGE - 1, c)


def on_device(amplitudes, block_rows, recoupling, interaction):
    amp = amplitudes.reshape(ROWS, Q)
    inter = interaction.reshape(NY * ROWS, ROWS)
    scratch = []
    for w in WIDTHS:
        scratch += [pltpu.VMEM((ROWS, w), BF)] * len(BUFS)
        scratch += [pltpu.VMEM((NY * ROWS, w), BF), pltpu.VMEM(((NY - 1) * ROWS, w), BF)]
    scratch += [pltpu.VMEM((ROWS, Q), BF), pltpu.VMEM((NY * ROWS, ROWS), BF), pltpu.VMEM((NCHAN, NCHAN), BF)]
    scratch += [pltpu.VMEM((ROWS, ROWS), BF)] * 4
    scratch += [pltpu.SemaphoreType.DMA((N_STAGE, C)), pltpu.SemaphoreType.DMA((N_STAGE, C))]
    scratch += [pltpu.SemaphoreType.DMA((C + 2,))]
    out = pl.pallas_call(
        kernel,
        out_shape=jax.ShapeDtypeStruct((ROWS, Q), BF),
        in_specs=[pl.BlockSpec(memory_space=pltpu.SMEM)] + [pl.BlockSpec(memory_space=pl.ANY)] * 3,
        out_specs=pl.BlockSpec(memory_space=pltpu.VMEM),
        scratch_shapes=scratch,
        compiler_params=pltpu.CompilerParams(
            collective_id=0, has_side_effects=True, vmem_limit_bytes=44 * 1024 * 1024
        ),
        cost_estimate=pl.CostEstimate(flops=4 * 10**9, bytes_accessed=4 * 10**6, transcendentals=0),
    )(block_rows, *[pltpu.with_memory_space_constraint(v, pltpu.HBM) for v in (amp, recoupling, inter)])
    rows = lax.axis_index("row") * ROWS + lax.iota(jnp.int32, ROWS)
    live = (rows[:, None] < block_rows[None, :])[:, :, None]
    return jnp.where(live, out.reshape(ROWS, 1, Q), jnp.zeros((), BF))


def solution(mesh):
    return jax.shard_map(
        on_device,
        mesh=mesh,
        in_specs=(P("row", "chan", None), P("chan"), P(), P(None, "chan", "row")),
        out_specs=P("row", "chan", None),
        check_vma=False,
    )
```

```python
import jax
import jax.numpy as jnp
from jax import lax
from jax.experimental import pallas as pl
from jax.experimental.pallas import tpu as pltpu
from jax.sharding import PartitionSpec as P

MESH = pl.DeviceIdType.MESH
BF = jnp.bfloat16
F32 = jnp.float32

NX, NZ, NC, NY = 4, 16, 2, 4
NG = NX * NC
NCHAN = NG * NZ
ROWS = 512
SUB = ROWS // NCHAN
GB, ZB = ROWS // NG, ROWS // NZ
Q = 640
WIDTHS = (128,) * 5
STARTS = tuple(sum(WIDTHS[:i]) for i in range(len(WIDTHS)))
C = len(WIDTHS)

FIRST = 3

ORDER = (
    (0, 0), (0, 1), (0, 2), (1, 0), (0, 3), (2, 0), (1, 1), (0, 4), (2, 1), (1, 2),
    (3, 0), (2, 2), (1, 3), (3, 1), (2, 3), (1, 4), (3, 2), (2, 4), (4, 0), (3, 3),
    (4, 1), (3, 4), (4, 2), (5, 0), (4, 3), (5, 1), (4, 4), (5, 2), (6, 0), (5, 3),
    (7, 0), (6, 1), (5, 4), (7, 1), (6, 2), (8, 0), (7, 2), (6, 3), (8, 1), (7, 3),
    (6, 4), (8, 2), (7, 4), (9, 0), (8, 3), (9, 1), (8, 4), (9, 2), (9, 3), (9, 4),
)

BUFS = ("z1", "z1r", "x1", "x1r", "x2", "x2r", "z2", "z2r", "z3", "z3r", "x3", "x3r", "x4", "x4r", "z4")
N_STAGE = 9


def chan_of_row(r):
    g, z = r // GB, (r // SUB) % NZ
    return ((g // NC) * NZ + z) * NC + g % NC


def dot(a, b):
    return lax.dot_general(a, b, (((1,), (0,)), ((), ())), preferred_element_type=F32)


def dot_nt(a, b):
    return lax.dot_general(a, b, (((1,), (1,)), ((), ())), preferred_element_type=F32)


def kernel(length, amp_any, rec_any, int_any, out_any, *refs):
    bufs = []
    n = len(BUFS) + 2
    for c in range(C):
        bufs.append(dict(zip(BUFS + ("ts", "tr"), refs[c * n : (c + 1) * n])))
    amp, inter, rec, k1, k2, p1, p2, recv, send, load = refs[C * n :]

    loads = []
    for c in range(C):
        cols = pl.ds(STARTS[c], WIDTHS[c])
        loads.append(pltpu.make_async_copy(amp_any.at[:, cols], amp.at[:, cols], load.at[c]))
    loads.append(pltpu.make_async_copy(rec_any, rec, load.at[C]))
    loads.append(pltpu.make_async_copy(int_any, inter, load.at[C + 1]))
    loads[0].start()

    chan, y = lax.axis_index("chan"), lax.axis_index("row")
    core, z, x = chan % NC, (chan // NC) % NZ, chan // (NC * NZ)
    g = x * NC + core

    def at_group(peer):
        return (((peer // NC) * NZ + z) * NC + peer % NC, y)

    def at_z(peer):
        return ((x * NZ + peer) * NC + core, y)

    def at_y(peer):
        return (chan, peer)

    barrier = pltpu.get_barrier_semaphore()

    def hail(count, me, where):
        for i in range(1, count):
            pl.semaphore_signal(barrier, inc=1, device_id=where((me + i) % count), device_id_type=MESH)

    hail(NZ, z, at_z)
    hail(NG, g, at_group)
    hail(NY, y, at_y)
    for copy in loads[1:]:
        copy.start()

    def mask_in(c):
        loads[c].wait()
        value = amp[:, pl.ds(STARTS[c], WIDTHS[c])]
        rows = lax.broadcasted_iota(jnp.int32, value.shape, 0)
        live = rows < length[0] - y * ROWS
        bufs[c]["z1"][...] = jnp.where(live, value.astype(F32), 0.0).astype(BF)

    def build():
        r = lax.broadcasted_iota(jnp.int32, (ROWS, NCHAN), 0)
        k = lax.broadcasted_iota(jnp.int32, (ROWS, NCHAN), 1)
        pick = (chan_of_row(r) == k).astype(F32).astype(BF)
        a = lax.broadcasted_iota(jnp.int32, (ROWS, ROWS), 0)
        b = lax.broadcasted_iota(jnp.int32, (ROWS, ROWS), 1)
        same = (a % SUB) == (b % SUB)
        there = ((a // SUB) % NZ) * ZB + (a // GB) * SUB + a % SUB
        p1[...] = (there == b).astype(F32).astype(BF)
        back = ((b // SUB) % NZ) * ZB + (b // GB) * SUB + b % SUB
        p2[...] = (back == a).astype(F32).astype(BF)
        loads[C].wait()
        coef = rec[...]
        k1[...] = jnp.where(same, dot_nt(dot(pick, coef).astype(BF), pick), 0.0).astype(BF)
        k2[...] = jnp.where(same, dot_nt(dot_nt(pick, coef).astype(BF), pick), 0.0).astype(BF)

    def swap(stage, c, src, dst, count, me, rows, where):
        own = pl.ds(pl.multiple_of(me * rows, rows), rows)
        pltpu.make_async_copy(src.at[own], dst.at[own], recv.at[stage, c]).start()

        def body(i, carry):
            if count == NZ:
                odd = i % 2
                peer = (me + NZ // 2 + (1 - odd) * (i // 2) - odd * ((i + 1) // 2)) % count
            else:
                peer = (me + i + 1) % count
            pltpu.make_async_remote_copy(
                src_ref=src.at[pl.ds(pl.multiple_of(peer * rows, rows), rows)],
                dst_ref=dst.at[own],
                send_sem=send.at[stage, c],
                recv_sem=recv.at[stage, c],
                device_id=where(peer),
                device_id_type=MESH,
            ).start()
            return carry

        lax.fori_loop(0, count - 1, body, 0)

    def swap_group(stage, c, src, dst):
        swap(stage, c, bufs[c][src], bufs[c][dst], NG, g, GB, at_group)

    def out_cols(c):
        return out_any.at[:, pl.ds(STARTS[c], WIDTHS[c])]

    def swap_z(stage, c, src, dst):
        to = bufs[c][dst] if dst else out_cols(c)
        swap(stage, c, bufs[c][src], to, NZ, z, ZB, at_z)

    own_z = pl.ds(pl.multiple_of(z * ZB, ZB), ZB)

    def give_back(c, begin, end):
        def body(peer, carry):
            @pl.when(peer != z)
            def _():
                pltpu.make_async_remote_copy(
                    src_ref=bufs[c]["z4"].at[pl.ds(pl.multiple_of(peer * ZB, ZB), ZB)],
                    dst_ref=out_cols(c).at[own_z],
                    send_sem=send.at[8, c],
                    recv_sem=recv.at[8, c],
                    device_id=at_z(peer),
                    device_id_type=MESH,
                ).start()

            return carry

        lax.fori_loop(begin, end, body, 0)

    def arrived(stage, c, dst):
        ref = bufs[c][dst] if dst else out_cols(c)
        pltpu.make_async_copy(ref, ref, recv.at[stage, c]).wait()
        return ref

    def step(s, c):
        b = bufs[c]
        if s == 0:
            if c:
                mask_in(c)
            swap_z(0, c, "z1", "z1r")
        elif s == 1:
            b["x1"][...] = dot(p1[...], arrived(0, c, "z1r")[...]).astype(BF)
            swap_group(1, c, "x1", "x1r")
        elif s == 2:
            b["x2"][...] = dot(k1[...], arrived(1, c, "x1r")[...]).astype(BF)
            swap_group(2, c, "x2", "x2r")
        elif s == 3:
            b["z2"][...] = dot(p2[...], arrived(2, c, "x2r")[...]).astype(BF)
            swap_z(3, c, "z2", "z2r")
        elif s == 4:
            cross = arrived(3, c, "z2r")
            if c == 0:
                loads[C + 1].wait()

            def body(i, carry):
                peer = (y + 1 + i) % NY
                rows = pl.ds(pl.multiple_of(peer * ROWS, ROWS), ROWS)
                b["ts"][rows, :] = dot(inter[rows, :], cross[...]).astype(BF)

                @pl.when(i < NY - 1)
                def _():
                    pltpu.make_async_remote_copy(
                        src_ref=b["ts"].at[rows],
                        dst_ref=b["tr"].at[pl.ds(pl.multiple_of(i * ROWS, ROWS), ROWS)],
                        send_sem=send.at[4, c],
                        recv_sem=recv.at[4, c],
                        device_id=at_y(peer),
                        device_id_type=MESH,
                    ).start()

                return carry

            lax.fori_loop(0, NY, body, 0)
        elif s == 5:
            tr = arrived(4, c, "tr")
            total = b["ts"][pl.ds(pl.multiple_of(y * ROWS, ROWS), ROWS), :].astype(F32)
            for i in range(NY - 1):
                total = total + tr[pl.ds(i * ROWS, ROWS), :].astype(F32)
            b["z3"][...] = total.astype(BF)
            swap_z(5, c, "z3", "z3r")
        elif s == 6:
            b["x3"][...] = dot(p1[...], arrived(5, c, "z3r")[...]).astype(BF)
            swap_group(6, c, "x3", "x3r")
        elif s == 7:
            b["x4"][...] = dot(k2[...], arrived(6, c, "x3r")[...]).astype(BF)
            swap_group(7, c, "x4", "x4r")
        elif s == 8:
            b["z4"][...] = dot(p2[...], arrived(7, c, "x4r")[...]).astype(BF)
            if c < C - 2:
                swap_z(8, c, "z4", None)
            else:
                pltpu.make_async_copy(b["z4"].at[own_z], out_cols(c).at[own_z], recv.at[8, c]).start()
                give_back(c, 0, FIRST)
            if c == C - 1:
                give_back(C - 2, FIRST, NZ)
                give_back(C - 1, FIRST, NZ)
        else:
            arrived(8, c, None)

    def sent(stage, c):
        rows = ROWS * (NY - 1) if stage == 4 else ROWS - (ZB if stage in (0, 3, 5, 8) else GB)
        part = bufs[c]["ts"].at[pl.ds(0, rows)]
        pltpu.make_async_copy(part, part, send.at[stage, c]).wait()

    mask_in(0)
    pl.semaphore_wait(barrier, NG + NZ + NY - 3)
    for i, (s, c) in enumerate(ORDER):
        step(s, c)
        if s >= 2:
            sent(s - 2, c)
        if i == 1:
            build()
    for c in range(C):
        sent(N_STAGE - 1, c)


def on_device(amplitudes, block_rows, recoupling, interaction):
    amp = amplitudes.reshape(ROWS, Q)
    inter = interaction.reshape(NY * ROWS, ROWS)
    scratch = []
    for w in WIDTHS:
        scratch += [pltpu.VMEM((ROWS, w), BF)] * len(BUFS)
        scratch += [pltpu.VMEM((NY * ROWS, w), BF), pltpu.VMEM(((NY - 1) * ROWS, w), BF)]
    scratch += [pltpu.VMEM((ROWS, Q), BF), pltpu.VMEM((NY * ROWS, ROWS), BF), pltpu.VMEM((NCHAN, NCHAN), BF)]
    scratch += [pltpu.VMEM((ROWS, ROWS), BF)] * 4
    scratch += [pltpu.SemaphoreType.DMA((N_STAGE, C)), pltpu.SemaphoreType.DMA((N_STAGE, C))]
    scratch += [pltpu.SemaphoreType.DMA((C + 2,))]
    out = pl.pallas_call(
        kernel,
        out_shape=jax.ShapeDtypeStruct((ROWS, Q), BF),
        in_specs=[pl.BlockSpec(memory_space=pltpu.SMEM)] + [pl.BlockSpec(memory_space=pl.ANY)] * 3,
        out_specs=pl.BlockSpec(memory_space=pltpu.VMEM),
        scratch_shapes=scratch,
        compiler_params=pltpu.CompilerParams(
            collective_id=0, has_side_effects=True, vmem_limit_bytes=44 * 1024 * 1024
        ),
        cost_estimate=pl.CostEstimate(flops=4 * 10**9, bytes_accessed=4 * 10**6, transcendentals=0),
    )(block_rows, *[pltpu.with_memory_space_constraint(v, pltpu.HBM) for v in (amp, recoupling, inter)])
    rows = lax.axis_index("row") * ROWS + lax.iota(jnp.int32, ROWS)
    live = (rows[:, None] < block_rows[None, :])[:, :, None]
    return jnp.where(live, out.reshape(ROWS, 1, Q), jnp.zeros((), BF))


def solution(mesh):
    return jax.shard_map(
        on_device,
        mesh=mesh,
        in_specs=(P("row", "chan", None), P("chan"), P(), P(None, "chan", "row")),
        out_specs=P("row", "chan", None),
        check_vma=False,
    )
```

```python
import jax
import jax.numpy as jnp
from jax import lax
from jax.experimental import pallas as pl
from jax.experimental.pallas import tpu as pltpu
from jax.sharding import PartitionSpec as P

MESH = pl.DeviceIdType.MESH
BF = jnp.bfloat16
F32 = jnp.float32

NX, NZ, NC, NY = 4, 16, 2, 4
NG = NX * NC
NCHAN = NG * NZ
ROWS = 512
SUB = ROWS // NCHAN
GB, ZB = ROWS // NG, ROWS // NZ
Q = 640
WIDTHS = (128,) * 5
STARTS = tuple(sum(WIDTHS[:i]) for i in range(len(WIDTHS)))
C = len(WIDTHS)

FIRST, SECOND = 2, 5

ORDER = (
    (0, 0), (0, 1), (0, 2), (1, 0), (0, 3), (2, 0), (1, 1), (0, 4), (2, 1), (1, 2),
    (3, 0), (2, 2), (1, 3), (3, 1), (2, 3), (1, 4), (3, 2), (2, 4), (4, 0), (3, 3),
    (4, 1), (3, 4), (4, 2), (5, 0), (4, 3), (5, 1), (4, 4), (5, 2), (6, 0), (5, 3),
    (7, 0), (6, 1), (5, 4), (7, 1), (6, 2), (8, 0), (7, 2), (6, 3), (8, 1), (7, 3),
    (6, 4), (8, 2), (7, 4), (9, 0), (8, 3), (9, 1), (8, 4), (9, 2), (9, 3), (9, 4),
)

BUFS = ("z1", "z1r", "x1", "x1r", "x2", "x2r", "z2", "z2r", "z3", "z3r", "x3", "x3r", "x4", "x4r", "z4")
N_STAGE = 9


def chan_of_row(r):
    g, z = r // GB, (r // SUB) % NZ
    return ((g // NC) * NZ + z) * NC + g % NC


def dot(a, b):
    return lax.dot_general(a, b, (((1,), (0,)), ((), ())), preferred_element_type=F32)


def dot_nt(a, b):
    return lax.dot_general(a, b, (((1,), (1,)), ((), ())), preferred_element_type=F32)


def kernel(length, amp_any, rec_any, int_any, out_any, *refs):
    bufs = []
    n = len(BUFS) + 2
    for c in range(C):
        bufs.append(dict(zip(BUFS + ("ts", "tr"), refs[c * n : (c + 1) * n])))
    amp, inter, rec, k1, k2, p1, p2, recv, send, load = refs[C * n :]

    loads = []
    for c in range(C):
        cols = pl.ds(STARTS[c], WIDTHS[c])
        loads.append(pltpu.make_async_copy(amp_any.at[:, cols], amp.at[:, cols], load.at[c]))
    loads.append(pltpu.make_async_copy(rec_any, rec, load.at[C]))
    loads.append(pltpu.make_async_copy(int_any, inter, load.at[C + 1]))
    loads[0].start()

    chan, y = lax.axis_index("chan"), lax.axis_index("row")
    core, z, x = chan % NC, (chan // NC) % NZ, chan // (NC * NZ)
    g = x * NC + core

    def at_group(peer):
        return (((peer // NC) * NZ + z) * NC + peer % NC, y)

    def at_z(peer):
        return ((x * NZ + peer) * NC + core, y)

    def at_y(peer):
        return (chan, peer)

    barrier = pltpu.get_barrier_semaphore()

    def hail(count, me, where):
        for i in range(1, count):
            pl.semaphore_signal(barrier, inc=1, device_id=where((me + i) % count), device_id_type=MESH)

    hail(NZ, z, at_z)
    hail(NG, g, at_group)
    hail(NY, y, at_y)
    for copy in loads[1:]:
        copy.start()

    def mask_in(c):
        loads[c].wait()
        value = amp[:, pl.ds(STARTS[c], WIDTHS[c])]
        rows = lax.broadcasted_iota(jnp.int32, value.shape, 0)
        live = rows < length[0] - y * ROWS
        bufs[c]["z1"][...] = jnp.where(live, value.astype(F32), 0.0).astype(BF)

    def build():
        r = lax.broadcasted_iota(jnp.int32, (ROWS, NCHAN), 0)
        k = lax.broadcasted_iota(jnp.int32, (ROWS, NCHAN), 1)
        pick = (chan_of_row(r) == k).astype(F32).astype(BF)
        a = lax.broadcasted_iota(jnp.int32, (ROWS, ROWS), 0)
        b = lax.broadcasted_iota(jnp.int32, (ROWS, ROWS), 1)
        same = (a % SUB) == (b % SUB)
        there = ((a // SUB) % NZ) * ZB + (a // GB) * SUB + a % SUB
        p1[...] = (there == b).astype(F32).astype(BF)
        back = ((b // SUB) % NZ) * ZB + (b // GB) * SUB + b % SUB
        p2[...] = (back == a).astype(F32).astype(BF)
        loads[C].wait()
        coef = rec[...]
        k1[...] = jnp.where(same, dot_nt(dot(pick, coef).astype(BF), pick), 0.0).astype(BF)
        k2[...] = jnp.where(same, dot_nt(dot_nt(pick, coef).astype(BF), pick), 0.0).astype(BF)

    def swap(stage, c, src, dst, count, me, rows, where):
        own = pl.ds(pl.multiple_of(me * rows, rows), rows)
        pltpu.make_async_copy(src.at[own], dst.at[own], recv.at[stage, c]).start()

        def body(i, carry):
            if count == NZ:
                odd = i % 2
                peer = (me + NZ // 2 + (1 - odd) * (i // 2) - odd * ((i + 1) // 2)) % count
            else:
                peer = (me + i + 1) % count
            pltpu.make_async_remote_copy(
                src_ref=src.at[pl.ds(pl.multiple_of(peer * rows, rows), rows)],
                dst_ref=dst.at[own],
                send_sem=send.at[stage, c],
                recv_sem=recv.at[stage, c],
                device_id=where(peer),
                device_id_type=MESH,
            ).start()
            return carry

        lax.fori_loop(0, count - 1, body, 0)

    def swap_group(stage, c, src, dst):
        swap(stage, c, bufs[c][src], bufs[c][dst], NG, g, GB, at_group)

    def out_cols(c):
        return out_any.at[:, pl.ds(STARTS[c], WIDTHS[c])]

    def swap_z(stage, c, src, dst):
        to = bufs[c][dst] if dst else out_cols(c)
        swap(stage, c, bufs[c][src], to, NZ, z, ZB, at_z)

    own_z = pl.ds(pl.multiple_of(z * ZB, ZB), ZB)

    def give_back(c, begin, end):
        def body(peer, carry):
            @pl.when(peer != z)
            def _():
                pltpu.make_async_remote_copy(
                    src_ref=bufs[c]["z4"].at[pl.ds(pl.multiple_of(peer * ZB, ZB), ZB)],
                    dst_ref=out_cols(c).at[own_z],
                    send_sem=send.at[8, c],
                    recv_sem=recv.at[8, c],
                    device_id=at_z(peer),
                    device_id_type=MESH,
                ).start()

            return carry

        lax.fori_loop(begin, end, body, 0)

    def arrived(stage, c, dst):
        ref = bufs[c][dst] if dst else out_cols(c)
        pltpu.make_async_copy(ref, ref, recv.at[stage, c]).wait()
        return ref

    def step(s, c):
        b = bufs[c]
        if s == 0:
            if c:
                mask_in(c)
            swap_z(0, c, "z1", "z1r")
        elif s == 1:
            b["x1"][...] = dot(p1[...], arrived(0, c, "z1r")[...]).astype(BF)
            swap_group(1, c, "x1", "x1r")
        elif s == 2:
            b["x2"][...] = dot(k1[...], arrived(1, c, "x1r")[...]).astype(BF)
            swap_group(2, c, "x2", "x2r")
        elif s == 3:
            b["z2"][...] = dot(p2[...], arrived(2, c, "x2r")[...]).astype(BF)
            swap_z(3, c, "z2", "z2r")
        elif s == 4:
            cross = arrived(3, c, "z2r")
            if c == 0:
                loads[C + 1].wait()

            def body(i, carry):
                peer = (y + 1 + i) % NY
                rows = pl.ds(pl.multiple_of(peer * ROWS, ROWS), ROWS)
                b["ts"][rows, :] = dot(inter[rows, :], cross[...]).astype(BF)

                @pl.when(i < NY - 1)
                def _():
                    pltpu.make_async_remote_copy(
                        src_ref=b["ts"].at[rows],
                        dst_ref=b["tr"].at[pl.ds(pl.multiple_of(i * ROWS, ROWS), ROWS)],
                        send_sem=send.at[4, c],
                        recv_sem=recv.at[4, c],
                        device_id=at_y(peer),
                        device_id_type=MESH,
                    ).start()

                return carry

            lax.fori_loop(0, NY, body, 0)
        elif s == 5:
            tr = arrived(4, c, "tr")
            total = b["ts"][pl.ds(pl.multiple_of(y * ROWS, ROWS), ROWS), :].astype(F32)
            for i in range(NY - 1):
                total = total + tr[pl.ds(i * ROWS, ROWS), :].astype(F32)
            b["z3"][...] = total.astype(BF)
            swap_z(5, c, "z3", "z3r")
        elif s == 6:
            b["x3"][...] = dot(p1[...], arrived(5, c, "z3r")[...]).astype(BF)
            swap_group(6, c, "x3", "x3r")
        elif s == 7:
            b["x4"][...] = dot(k2[...], arrived(6, c, "x3r")[...]).astype(BF)
            swap_group(7, c, "x4", "x4r")
        elif s == 8:
            b["z4"][...] = dot(p2[...], arrived(7, c, "x4r")[...]).astype(BF)
            if c < C - 2:
                swap_z(8, c, "z4", None)
            else:
                pltpu.make_async_copy(b["z4"].at[own_z], out_cols(c).at[own_z], recv.at[8, c]).start()
                give_back(c, 0, FIRST)
            if c == C - 1:
                for begin, end in ((FIRST, SECOND), (SECOND, NZ)):
                    give_back(C - 2, begin, end)
                    give_back(C - 1, begin, end)
        else:
            arrived(8, c, None)

    def sent(stage, c):
        rows = ROWS * (NY - 1) if stage == 4 else ROWS - (ZB if stage in (0, 3, 5, 8) else GB)
        part = bufs[c]["ts"].at[pl.ds(0, rows)]
        pltpu.make_async_copy(part, part, send.at[stage, c]).wait()

    mask_in(0)
    pl.semaphore_wait(barrier, NG + NZ + NY - 3)
    for i, (s, c) in enumerate(ORDER):
        step(s, c)
        if s >= 2:
            sent(s - 2, c)
        if i == 1:
            build()
    for c in range(C):
        sent(N_STAGE - 1, c)


def on_device(amplitudes, block_rows, recoupling, interaction):
    amp = amplitudes.reshape(ROWS, Q)
    inter = interaction.reshape(NY * ROWS, ROWS)
    scratch = []
    for w in WIDTHS:
        scratch += [pltpu.VMEM((ROWS, w), BF)] * len(BUFS)
        scratch += [pltpu.VMEM((NY * ROWS, w), BF), pltpu.VMEM(((NY - 1) * ROWS, w), BF)]
    scratch += [pltpu.VMEM((ROWS, Q), BF), pltpu.VMEM((NY * ROWS, ROWS), BF), pltpu.VMEM((NCHAN, NCHAN), BF)]
    scratch += [pltpu.VMEM((ROWS, ROWS), BF)] * 4
    scratch += [pltpu.SemaphoreType.DMA((N_STAGE, C)), pltpu.SemaphoreType.DMA((N_STAGE, C))]
    scratch += [pltpu.SemaphoreType.DMA((C + 2,))]
    out = pl.pallas_call(
        kernel,
        out_shape=jax.ShapeDtypeStruct((ROWS, Q), BF),
        in_specs=[pl.BlockSpec(memory_space=pltpu.SMEM)] + [pl.BlockSpec(memory_space=pl.ANY)] * 3,
        out_specs=pl.BlockSpec(memory_space=pltpu.VMEM),
        scratch_shapes=scratch,
        compiler_params=pltpu.CompilerParams(
            collective_id=0, has_side_effects=True, vmem_limit_bytes=44 * 1024 * 1024
        ),
        cost_estimate=pl.CostEstimate(flops=4 * 10**9, bytes_accessed=4 * 10**6, transcendentals=0),
    )(block_rows, *[pltpu.with_memory_space_constraint(v, pltpu.HBM) for v in (amp, recoupling, inter)])
    rows = lax.axis_index("row") * ROWS + lax.iota(jnp.int32, ROWS)
    live = (rows[:, None] < block_rows[None, :])[:, :, None]
    return jnp.where(live, out.reshape(ROWS, 1, Q), jnp.zeros((), BF))


def solution(mesh):
    return jax.shard_map(
        on_device,
        mesh=mesh,
        in_specs=(P("row", "chan", None), P("chan"), P(), P(None, "chan", "row")),
        out_specs=P("row", "chan", None),
        check_vma=False,
    )
```

```python
import jax
import jax.numpy as jnp
from jax import lax
from jax.experimental import pallas as pl
from jax.experimental.pallas import tpu as pltpu
from jax.sharding import PartitionSpec as P

MESH = pl.DeviceIdType.MESH
BF = jnp.bfloat16
F32 = jnp.float32

NX, NZ, NC, NY = 4, 16, 2, 4
NG = NX * NC
NCHAN = NG * NZ
ROWS = 512
SUB = ROWS // NCHAN
GB, ZB = ROWS // NG, ROWS // NZ
Q = 640
WIDTHS = (128,) * 5
STARTS = tuple(sum(WIDTHS[:i]) for i in range(len(WIDTHS)))
C = len(WIDTHS)

FIRST, SECOND = 2, 5

ORDER = (
    (0, 0), (0, 1), (0, 2), (1, 0), (0, 3), (2, 0), (1, 1), (0, 4), (2, 1), (1, 2),
    (3, 0), (2, 2), (1, 3), (3, 1), (2, 3), (1, 4), (3, 2), (2, 4), (4, 0), (3, 3),
    (4, 1), (3, 4), (4, 2), (5, 0), (4, 3), (5, 1), (4, 4), (5, 2), (6, 0), (5, 3),
    (7, 0), (6, 1), (5, 4), (7, 1), (6, 2), (8, 0), (7, 2), (6, 3), (8, 1), (7, 3),
    (6, 4), (8, 2), (7, 4), (8, 3), (8, 4), (9, 0), (9, 1), (9, 2), (9, 3), (9, 4),
)

BUFS = ("z1", "z1r", "x1", "x1r", "x2", "x2r", "z2", "z2r", "z3", "z3r", "x3", "x3r", "x4", "x4r", "z4")
N_STAGE = 9


def chan_of_row(r):
    g, z = r // GB, (r // SUB) % NZ
    return ((g // NC) * NZ + z) * NC + g % NC


def dot(a, b):
    return lax.dot_general(a, b, (((1,), (0,)), ((), ())), preferred_element_type=F32)


def dot_nt(a, b):
    return lax.dot_general(a, b, (((1,), (1,)), ((), ())), preferred_element_type=F32)


def kernel(length, amp_any, rec_any, int_any, out_any, *refs):
    bufs = []
    n = len(BUFS) + 2
    for c in range(C):
        bufs.append(dict(zip(BUFS + ("ts", "tr"), refs[c * n : (c + 1) * n])))
    amp, inter, rec, k1, k2, p1, p2, recv, send, load = refs[C * n :]

    loads = []
    for c in range(C):
        cols = pl.ds(STARTS[c], WIDTHS[c])
        loads.append(pltpu.make_async_copy(amp_any.at[:, cols], amp.at[:, cols], load.at[c]))
    loads.append(pltpu.make_async_copy(rec_any, rec, load.at[C]))
    loads.append(pltpu.make_async_copy(int_any, inter, load.at[C + 1]))
    loads[0].start()

    chan, y = lax.axis_index("chan"), lax.axis_index("row")
    core, z, x = chan % NC, (chan // NC) % NZ, chan // (NC * NZ)
    g = x * NC + core

    def at_group(peer):
        return (((peer // NC) * NZ + z) * NC + peer % NC, y)

    def at_z(peer):
        return ((x * NZ + peer) * NC + core, y)

    def at_y(peer):
        return (chan, peer)

    barrier = pltpu.get_barrier_semaphore()

    def hail(count, me, where):
        for i in range(1, count):
            pl.semaphore_signal(barrier, inc=1, device_id=where((me + i) % count), device_id_type=MESH)

    hail(NZ, z, at_z)
    hail(NG, g, at_group)
    hail(NY, y, at_y)
    for copy in loads[1:]:
        copy.start()

    def mask_in(c):
        loads[c].wait()
        value = amp[:, pl.ds(STARTS[c], WIDTHS[c])]
        rows = lax.broadcasted_iota(jnp.int32, value.shape, 0)
        live = rows < length[0] - y * ROWS
        bufs[c]["z1"][...] = jnp.where(live, value.astype(F32), 0.0).astype(BF)

    def build():
        r = lax.broadcasted_iota(jnp.int32, (ROWS, NCHAN), 0)
        k = lax.broadcasted_iota(jnp.int32, (ROWS, NCHAN), 1)
        pick = (chan_of_row(r) == k).astype(F32).astype(BF)
        a = lax.broadcasted_iota(jnp.int32, (ROWS, ROWS), 0)
        b = lax.broadcasted_iota(jnp.int32, (ROWS, ROWS), 1)
        same = (a % SUB) == (b % SUB)
        there = ((a // SUB) % NZ) * ZB + (a // GB) * SUB + a % SUB
        p1[...] = (there == b).astype(F32).astype(BF)
        back = ((b // SUB) % NZ) * ZB + (b // GB) * SUB + b % SUB
        p2[...] = (back == a).astype(F32).astype(BF)
        loads[C].wait()
        coef = rec[...]
        k1[...] = jnp.where(same, dot_nt(dot(pick, coef).astype(BF), pick), 0.0).astype(BF)
        k2[...] = jnp.where(same, dot_nt(dot_nt(pick, coef).astype(BF), pick), 0.0).astype(BF)

    def swap(stage, c, src, dst, count, me, rows, where):
        own = pl.ds(pl.multiple_of(me * rows, rows), rows)
        pltpu.make_async_copy(src.at[own], dst.at[own], recv.at[stage, c]).start()

        def body(i, carry):
            if count == NZ:
                odd = i % 2
                peer = (me + NZ // 2 + (1 - odd) * (i // 2) - odd * ((i + 1) // 2)) % count
            else:
                peer = (me + i + 1) % count
            pltpu.make_async_remote_copy(
                src_ref=src.at[pl.ds(pl.multiple_of(peer * rows, rows), rows)],
                dst_ref=dst.at[own],
                send_sem=send.at[stage, c],
                recv_sem=recv.at[stage, c],
                device_id=where(peer),
                device_id_type=MESH,
            ).start()
            return carry

        lax.fori_loop(0, count - 1, body, 0)

    def swap_group(stage, c, src, dst):
        swap(stage, c, bufs[c][src], bufs[c][dst], NG, g, GB, at_group)

    def out_cols(c):
        return out_any.at[:, pl.ds(STARTS[c], WIDTHS[c])]

    def swap_z(stage, c, src, dst):
        to = bufs[c][dst] if dst else out_cols(c)
        swap(stage, c, bufs[c][src], to, NZ, z, ZB, at_z)

    own_z = pl.ds(pl.multiple_of(z * ZB, ZB), ZB)

    def give_back(c, begin, end):
        def body(peer, carry):
            @pl.when(peer != z)
            def _():
                pltpu.make_async_remote_copy(
                    src_ref=bufs[c]["z4"].at[pl.ds(pl.multiple_of(peer * ZB, ZB), ZB)],
                    dst_ref=out_cols(c).at[own_z],
                    send_sem=send.at[8, c],
                    recv_sem=recv.at[8, c],
                    device_id=at_z(peer),
                    device_id_type=MESH,
                ).start()

            return carry

        lax.fori_loop(begin, end, body, 0)

    def arrived(stage, c, dst):
        ref = bufs[c][dst] if dst else out_cols(c)
        pltpu.make_async_copy(ref, ref, recv.at[stage, c]).wait()
        return ref

    def step(s, c):
        b = bufs[c]
        if s == 0:
            if c:
                mask_in(c)
            swap_z(0, c, "z1", "z1r")
        elif s == 1:
            b["x1"][...] = dot(p1[...], arrived(0, c, "z1r")[...]).astype(BF)
            swap_group(1, c, "x1", "x1r")
        elif s == 2:
            b["x2"][...] = dot(k1[...], arrived(1, c, "x1r")[...]).astype(BF)
            swap_group(2, c, "x2", "x2r")
        elif s == 3:
            b["z2"][...] = dot(p2[...], arrived(2, c, "x2r")[...]).astype(BF)
            swap_z(3, c, "z2", "z2r")
        elif s == 4:
            cross = arrived(3, c, "z2r")
            if c == 0:
                loads[C + 1].wait()

            def body(i, carry):
                peer = (y + 1 + i) % NY
                rows = pl.ds(pl.multiple_of(peer * ROWS, ROWS), ROWS)
                b["ts"][rows, :] = dot(inter[rows, :], cross[...]).astype(BF)

                @pl.when(i < NY - 1)
                def _():
                    pltpu.make_async_remote_copy(
                        src_ref=b["ts"].at[rows],
                        dst_ref=b["tr"].at[pl.ds(pl.multiple_of(i * ROWS, ROWS), ROWS)],
                        send_sem=send.at[4, c],
                        recv_sem=recv.at[4, c],
                        device_id=at_y(peer),
                        device_id_type=MESH,
                    ).start()

                return carry

            lax.fori_loop(0, NY, body, 0)
        elif s == 5:
            tr = arrived(4, c, "tr")
            total = b["ts"][pl.ds(pl.multiple_of(y * ROWS, ROWS), ROWS), :].astype(F32)
            for i in range(NY - 1):
                total = total + tr[pl.ds(i * ROWS, ROWS), :].astype(F32)
            b["z3"][...] = total.astype(BF)
            swap_z(5, c, "z3", "z3r")
        elif s == 6:
            b["x3"][...] = dot(p1[...], arrived(5, c, "z3r")[...]).astype(BF)
            swap_group(6, c, "x3", "x3r")
        elif s == 7:
            b["x4"][...] = dot(k2[...], arrived(6, c, "x3r")[...]).astype(BF)
            swap_group(7, c, "x4", "x4r")
        elif s == 8:
            b["z4"][...] = dot(p2[...], arrived(7, c, "x4r")[...]).astype(BF)
            if c < C - 2:
                swap_z(8, c, "z4", None)
            else:
                pltpu.make_async_copy(b["z4"].at[own_z], out_cols(c).at[own_z], recv.at[8, c]).start()
                give_back(c, 0, FIRST)
            if c == C - 1:
                for begin, end in ((FIRST, SECOND), (SECOND, NZ)):
                    give_back(C - 2, begin, end)
                    give_back(C - 1, begin, end)
        else:
            arrived(8, c, None)

    def sent(stage, c):
        rows = ROWS * (NY - 1) if stage == 4 else ROWS - (ZB if stage in (0, 3, 5, 8) else GB)
        part = bufs[c]["ts"].at[pl.ds(0, rows)]
        pltpu.make_async_copy(part, part, send.at[stage, c]).wait()

    mask_in(0)
    pl.semaphore_wait(barrier, NG + NZ + NY - 3)
    for i, (s, c) in enumerate(ORDER):
        step(s, c)
        if s >= 2:
            sent(s - 2, c)
        if i == 1:
            build()
    for c in range(C):
        sent(N_STAGE - 1, c)


def on_device(amplitudes, block_rows, recoupling, interaction):
    amp = amplitudes.reshape(ROWS, Q)
    inter = interaction.reshape(NY * ROWS, ROWS)
    scratch = []
    for w in WIDTHS:
        scratch += [pltpu.VMEM((ROWS, w), BF)] * len(BUFS)
        scratch += [pltpu.VMEM((NY * ROWS, w), BF), pltpu.VMEM(((NY - 1) * ROWS, w), BF)]
    scratch += [pltpu.VMEM((ROWS, Q), BF), pltpu.VMEM((NY * ROWS, ROWS), BF), pltpu.VMEM((NCHAN, NCHAN), BF)]
    scratch += [pltpu.VMEM((ROWS, ROWS), BF)] * 4
    scratch += [pltpu.SemaphoreType.DMA((N_STAGE, C)), pltpu.SemaphoreType.DMA((N_STAGE, C))]
    scratch += [pltpu.SemaphoreType.DMA((C + 2,))]
    out = pl.pallas_call(
        kernel,
        out_shape=jax.ShapeDtypeStruct((ROWS, Q), BF),
        in_specs=[pl.BlockSpec(memory_space=pltpu.SMEM)] + [pl.BlockSpec(memory_space=pl.ANY)] * 3,
        out_specs=pl.BlockSpec(memory_space=pltpu.VMEM),
        scratch_shapes=scratch,
        compiler_params=pltpu.CompilerParams(
            collective_id=0, has_side_effects=True, vmem_limit_bytes=44 * 1024 * 1024
        ),
        cost_estimate=pl.CostEstimate(flops=4 * 10**9, bytes_accessed=4 * 10**6, transcendentals=0),
    )(block_rows, *[pltpu.with_memory_space_constraint(v, pltpu.HBM) for v in (amp, recoupling, inter)])
    rows = lax.axis_index("row") * ROWS + lax.iota(jnp.int32, ROWS)
    live = (rows[:, None] < block_rows[None, :])[:, :, None]
    return jnp.where(live, out.reshape(ROWS, 1, Q), jnp.zeros((), BF))


def solution(mesh):
    return jax.shard_map(
        on_device,
        mesh=mesh,
        in_specs=(P("row", "chan", None), P("chan"), P(), P(None, "chan", "row")),
        out_specs=P("row", "chan", None),
        check_vma=False,
    )
```
